32 devices in a mesh: dp: 8 (over z, y), ctx: 4 (over x, core).
Axes of the slice: x: 2, y: 2, z: 4, core: 2. Of those that a mesh axis runs over, the one named last changes fastest.
Arguments:
- queries_q: bfloat16 [8, 512, 1792], P('dp', 'ctx'), may hold values from -5 to 5
- keys: bfloat16 [8, 512, 256], P('dp', 'ctx'), may hold values from -5 to 5
- values: bfloat16 [8, 512, 256], P('dp', 'ctx'), may hold values from -6 to 6
- lengths: int32 [8, 4], P('dp'), may hold values from 1 to 384, 512 in all within a row
- query_emb: bfloat16 [1024, 1792], P('dp'), may hold values from -6 to 6
- positive: int32 [1024], P('dp'), may hold values from 0 to 31
Outputs:
- query_grad: float32 [1024, 1792], P('dp')
- grad_queries: bfloat16 [8, 512, 1792], P('dp', 'ctx')
- grad_keys: bfloat16 [8, 512, 256], P('dp', 'ctx')
- grad_values: bfloat16 [8, 512, 256], P('dp', 'ctx')
The draws below stay inside these ranges and needn't reach their ends.
Inputs may be any that keep to these rules, and one draw needn't show every extreme that they name: The 4 lengths of each row sum to 512, and the longest is 384.
All inputs are finite; a program needn't handle non-finite values.
Results may differ from the reference program's by a relative error of at most 0.012.
The reference program's roundings to bfloat16 on the way count: a program that leaves them out, or rounds other values in their place, can miss the bound.
Values may be sent and summed in bfloat16 or wider, within the bound.
A program may use at most 64 MiB of HBM per device.

```python
import math
import jax
import jax.numpy as jnp
import numpy as np
from jax import lax

HEAD_DIM = 128
HEADS = 14
KV_HEADS = 2
DOCS = 4
ROWS = 8
SEQ = 512
EMB = 1792
KVW = 256
NQ = 1024
NDOC = 32
N_CTX = 4


def draw_queries_q(key, part):
    key = jax.random.fold_in(key, 5)
    per_group = HEADS // KV_HEADS
    draw_shape = (ROWS, SEQ, KV_HEADS, per_group, HEAD_DIM)
    seed_sample = jnp.clip(jax.random.normal(key, draw_shape, jnp.float32), -4.0, 4.0)
    return seed_sample.reshape(ROWS, SEQ, HEADS * HEAD_DIM).astype(jnp.bfloat16)


def draw_keys(key, part):
    key = jax.random.fold_in(key, 9)
    draw_shape = (ROWS, SEQ, KV_HEADS, HEAD_DIM)
    seed_sample = jnp.clip(jax.random.normal(key, draw_shape, jnp.float32), -4.0, 4.0)
    return seed_sample.reshape(ROWS, SEQ, KV_HEADS * HEAD_DIM).astype(jnp.bfloat16)


def place_ends(drawn, rng, low, largest):
    extent = drawn.shape
    place = [jax.random.randint(jax.random.fold_in(rng, axis), (), 0, extent[axis]) for axis in range(len(extent))]
    drawn = drawn.at[tuple(place)].set(low)
    longest = extent.index(max(extent))
    place[longest] = (place[longest] + 1) % extent[longest]
    return drawn.at[tuple(place)].set(largest)


def block_levels(own_key, extent, cuts, low, largest):
    def one(axis_at, blocks):
        draws = jax.random.uniform(jax.random.fold_in(jax.random.fold_in(own_key, 6), axis_at), (blocks,), jnp.float32, low / len(cuts), largest / len(cuts))
        return jnp.repeat(jnp.exp(draws), extent[axis_at] // blocks).reshape((-1,) + (1,) * (len(extent) - axis_at - 1))

    level = one(*cuts[0])
    for cut in cuts[1:]:
        level = level * one(*cut)
    return level


def length_profile(amount, total, bound, skew):
    weights = [(1 << 20) // math.isqrt(rank ** skew) + 1 for rank in range(2, amount + 1)]
    spare, given = total - bound - (amount - 1), [1] * (amount - 1)
    while spare > 0:
        candidates = [i for i in range(amount - 1) if given[i] < bound]
        whole, budget = sum([weights[i] for i in candidates]), spare
        for i in candidates:
            more = min(bound - given[i], max(1, budget * weights[i] // whole), spare)
            given[i] = given[i] + more
            spare = spare - more
    return np.array([bound] + given)


def ragged(key, amount, total, reach, slope):
    if amount == 2:
        one = jax.random.randint(key, (), max(1, total - reach), min(reach, total - 1) + 1)
        return jnp.stack([one, total - one])
    sizes = jnp.asarray(length_profile(amount, total, reach, slope), jnp.int32)
    pairs = (amount - 1) // 2
    giver, receiver = sizes[1:1 + 2 * pairs:2], sizes[2:2 + 2 * pairs:2]
    slack = jnp.minimum(giver - 1, reach - receiver)
    passed = jax.random.randint(jax.random.fold_in(key, 1), (pairs,), 0, 1 << 20) % (slack + 1)
    sizes = sizes.at[1:1 + 2 * pairs:2].set(giver - passed).at[2:2 + 2 * pairs:2].set(receiver + passed)
    return sizes[jax.random.permutation(jax.random.fold_in(key, 2), amount)]


def noise(own_key, dims, scale, limit, cuts=(), kind=jnp.bfloat16):
    entries = scale * jax.random.normal(own_key, dims, jnp.float32)
    if cuts:
        entries = entries * block_levels(own_key, dims, cuts, -0.22, 0.18)
    return jnp.clip(entries, -limit, limit).astype(kind)


def setup_inputs(seed: int = 0) -> dict:
    seeds = jax.random.split(jax.random.key(seed), 7)
    return {
        "queries_q": draw_queries_q(jax.random.fold_in(seeds[6], 71), 0),
        "keys": draw_keys(jax.random.fold_in(seeds[6], 71), 0),
        "values": noise(seeds[2], (ROWS, SEQ, KVW), 1.0, 6.0, ((0, 8), (1, 4))),
        "lengths": jax.vmap(lambda own: ragged(own, DOCS, SEQ, SEQ - SEQ // 4, 2))(jax.random.split(seeds[3], ROWS)).reshape((ROWS, DOCS)).astype(jnp.int32),
        "query_emb": noise(seeds[4], (NQ, EMB), 1.0, 6.0, ((0, 8),)),
        "positive": place_ends(jax.random.randint(seeds[5], (NQ,), 0, NDOC), jax.random.fold_in(seeds[5], 1), 0, NDOC - 1).astype(jnp.int32),
    }


INVERSE_TEMPER = 0.05
EPSILON = 1e-06
FULL_ACCURACY = lax.Precision.HIGHEST

def document_ids(lengths_row, positions):
    doc_ends = jnp.cumsum(lengths_row)
    return lax.optimization_barrier(jnp.sum((positions[:, None] >= doc_ends[None, :]).astype(jnp.int32), axis=1))

def rounded(values_in):
    return lax.optimization_barrier(values_in.astype(jnp.bfloat16)).astype(jnp.float32)

def rescale_back(inverse, unit_vec, upstream):
    inner_sum = lax.optimization_barrier(jnp.sum(unit_vec * upstream, axis=1, keepdims=True))
    return inverse * (upstream - unit_vec * inner_sum)

def reference(queries_q, keys, values, lengths, query_emb, positive):
    seq_len = queries_q.shape[1]
    tok_rows = seq_len // N_CTX
    per_group = HEADS // KV_HEADS
    factor = HEAD_DIM ** (-0.5)
    positions = jnp.arange(seq_len, dtype=jnp.int32)
    doc_index = jnp.arange(DOCS, dtype=jnp.int32)

    def scores_of(q_rows, k_row, row_start, doc_row):
        q_heads = q_rows.reshape(tok_rows, KV_HEADS, per_group, HEAD_DIM).astype(jnp.float32)
        k_heads = k_row.reshape(seq_len, KV_HEADS, HEAD_DIM).astype(jnp.float32)
        raw_scores = jnp.einsum('tgqd,sgd->gqts', q_heads, k_heads) * factor
        query_doc = lax.dynamic_slice_in_dim(doc_row, row_start, tok_rows, 0)
        query_pos = row_start + jnp.arange(tok_rows, dtype=jnp.int32)
        allowed = (query_doc[:, None] == doc_row[None, :]) & (positions[None, :] <= query_pos[:, None])
        return jnp.where(allowed, raw_scores, -jnp.inf)

    def forward_row(row_item):
        q_row, k_row, v_row, len_row = row_item
        doc_row = document_ids(len_row, positions)
        v_heads = v_row.reshape(seq_len, KV_HEADS, HEAD_DIM).astype(jnp.float32)

        def shard_pass(block_idx):
            row_start = block_idx * tok_rows
            q_rows = lax.dynamic_slice_in_dim(q_row, row_start, tok_rows, 0)
            scores = scores_of(q_rows, k_row, row_start, doc_row)
            row_top = lax.optimization_barrier(jnp.max(scores, axis=-1, keepdims=True))
            log_total = row_top + jnp.log(lax.optimization_barrier(jnp.sum(jnp.exp(scores - row_top), axis=-1, keepdims=True)))
            weights = rounded(jnp.exp(scores - log_total))
            out_rows = jnp.einsum('gqts,sgd->tgqd', weights, v_heads).reshape(tok_rows, EMB)
            return (out_rows, log_total)
        out_rows, log_rows = lax.map(shard_pass, jnp.arange(N_CTX, dtype=jnp.int32))
        attended = out_rows.reshape(seq_len, EMB)
        member = (doc_index[:, None] == doc_row[None, :]).astype(jnp.float32)
        doc_sum = jnp.dot(member, attended, precision=FULL_ACCURACY)
        return (attended, log_rows, doc_sum)
    attended, log_rows, doc_sums = lax.map(forward_row, (queries_q, keys, values, lengths))
    doc_len = lengths.reshape(-1).astype(jnp.float32)[:, None]
    doc_emb = doc_sums.reshape(-1, EMB) / doc_len
    doc_inv = lax.rsqrt(lax.optimization_barrier(jnp.sum(doc_emb * doc_emb, axis=1, keepdims=True)) + EPSILON)
    document_normalized = doc_emb * doc_inv
    query_f = query_emb.astype(jnp.float32)
    query_inv = lax.rsqrt(lax.optimization_barrier(jnp.sum(query_f * query_f, axis=1, keepdims=True)) + EPSILON)
    query_normalized = query_f * query_inv
    similarity_logits = jnp.dot(query_normalized, document_normalized.T, precision=FULL_ACCURACY) / INVERSE_TEMPER
    exp_logits = jnp.exp(similarity_logits)
    target = (jnp.arange(document_normalized.shape[0], dtype=jnp.int32)[None, :] == positive[:, None]).astype(jnp.float32)
    scaling_coefficient = exp_logits / lax.optimization_barrier(jnp.sum(exp_logits, axis=1, keepdims=True)) - target
    query_upstream_gradient = jnp.dot(scaling_coefficient, document_normalized, precision=FULL_ACCURACY) / INVERSE_TEMPER
    document_upstream_gradient = jnp.dot(scaling_coefficient.T, query_normalized, precision=FULL_ACCURACY) / INVERSE_TEMPER
    query_grad = rescale_back(query_inv, query_normalized, query_upstream_gradient)
    passage_derivative = (rescale_back(doc_inv, document_normalized, document_upstream_gradient) / doc_len).reshape(-1, DOCS, EMB)

    def backward_row(row_item):
        q_row, k_row, v_row, len_row, attended_row, log_row, grad_row = row_item
        doc_row = document_ids(len_row, positions)
        member = (doc_index[:, None] == doc_row[None, :]).astype(jnp.float32)
        out_grad = jnp.dot(member.T, grad_row, precision=FULL_ACCURACY)
        k_heads = k_row.reshape(seq_len, KV_HEADS, HEAD_DIM).astype(jnp.float32)
        v_heads = v_row.reshape(seq_len, KV_HEADS, HEAD_DIM).astype(jnp.float32)

        def shard_pass(carry, block_idx):
            key_acc, value_acc = carry
            row_start = block_idx * tok_rows
            q_rows = lax.dynamic_slice_in_dim(q_row, row_start, tok_rows, 0)
            q_heads = q_rows.reshape(tok_rows, KV_HEADS, per_group, HEAD_DIM).astype(jnp.float32)
            up_rows = lax.dynamic_slice_in_dim(out_grad, row_start, tok_rows, 0)
            att_rows = lax.dynamic_slice_in_dim(attended_row, row_start, tok_rows, 0)
            out_heads = rounded(up_rows).reshape(tok_rows, KV_HEADS, per_group, HEAD_DIM)
            row_delta = lax.optimization_barrier(jnp.sum((up_rows * att_rows).reshape(tok_rows, KV_HEADS, per_group, HEAD_DIM), axis=-1))
            row_delta = jnp.transpose(row_delta, (1, 2, 0))[..., None]
            scores = scores_of(q_rows, k_row, row_start, doc_row)
            probability = jnp.exp(scores - log_row[block_idx])
            weights = rounded(probability)
            flow_grad = jnp.einsum('tgqd,sgd->gqts', out_heads, v_heads)
            score_grad = rounded(probability * (flow_grad - row_delta))
            grad_rows = (jnp.einsum('gqts,sgd->tgqd', score_grad, k_heads) * factor).astype(jnp.bfloat16)
            key_part = rounded(jnp.einsum('gqts,tgqd->sgd', score_grad, q_heads) * factor)
            value_part = rounded(jnp.einsum('gqts,tgqd->sgd', weights, out_heads))
            return ((key_acc + key_part, value_acc + value_part), grad_rows.reshape(tok_rows, EMB))
        empty_acc = jnp.zeros((seq_len, KV_HEADS, HEAD_DIM), jnp.float32)
        (key_acc, value_acc), grad_rows = lax.scan(shard_pass, (empty_acc, empty_acc), jnp.arange(N_CTX, dtype=jnp.int32))
        return (grad_rows.reshape(seq_len, EMB), key_acc.reshape(seq_len, KVW).astype(jnp.bfloat16), value_acc.reshape(seq_len, KVW).astype(jnp.bfloat16))
    grad_queries, grad_keys, grad_values = lax.map(backward_row, (queries_q, keys, values, lengths, attended, log_rows, passage_derivative))
    return (query_grad, grad_queries, grad_keys, grad_values)
```

```python
import functools

import jax
import jax.numpy as jnp
from jax import lax
from jax.experimental import pallas as pl
from jax.experimental.pallas import tpu as pltpu
from jax.sharding import PartitionSpec as P

HEAD_DIM = 128
HEADS = 14
KV_HEADS = 2
PER_GROUP = HEADS // KV_HEADS
DOCS = 4
WIRE = KV_HEADS * DOCS

SCALE_UP = 20.0
EPSILON = 1e-06
NEG = -1e30
F32 = jnp.float32
BF16 = jnp.bfloat16
MESH = pl.DeviceIdType.MESH


def dot_nn(a, b):
    return lax.dot_general(a, b, (((1,), (0,)), ((), ())), preferred_element_type=F32)


def dot_nt(a, b):
    return lax.dot_general(a, b, (((1,), (1,)), ((), ())), preferred_element_type=F32)


def dot_tn(a, b):
    return lax.dot_general(a, b, (((0,), (0,)), ((), ())), preferred_element_type=F32)


def split(x):
    high = x.astype(BF16)
    return high, (x - high.astype(F32)).astype(BF16)


def swap_halves(x):
    return jnp.concatenate([x[DOCS:], x[:DOCS]], axis=0)


def doc_row_sum(x):
    rows = jnp.sum(x, axis=1, keepdims=True)
    return rows + swap_halves(rows)


def kernel(
    n_ctx, n_dp,
    len_ref, q_ref, k_ref, v_ref, emb_ref, pos_ref,
    qg_ref, gq_ref, gk_ref, gv_ref,
    k_all, v_all, q_s, probs, att, bias, sums, units, terms, doc_hi, doc_lo,
    doc_grad, out_low, s_grad, weights, k_out, v_out, k_in, v_in,
    kv_send, kv_recv, sum_send, sum_recv, unit_send, unit_recv, term_send, term_recv,
    part_send, part_recv,
):
    me = lax.axis_index("ctx")
    row = lax.axis_index("dp")
    tok = q_ref.shape[1]
    seq = k_all.shape[0]
    emb = q_ref.shape[2]
    half = emb // 2
    factor = HEAD_DIM ** (-0.5)
    sibling = me + 1 - 2 * lax.rem(me, 2)

    def ctx_peer(t):
        return lax.rem(me + t, n_ctx)

    def dp_peer(t):
        return lax.rem(row + t, n_dp)

    def block(ref, idx):
        return ref.at[pl.ds(pl.multiple_of(idx * tok, tok), tok)]

    barrier = pltpu.get_barrier_semaphore()
    for t in range(1, n_ctx):
        pl.semaphore_signal(barrier, inc=1, device_id={"ctx": ctx_peer(t)}, device_id_type=MESH)
    for t in range(1, n_dp):
        pl.semaphore_signal(barrier, inc=1, device_id={"dp": dp_peer(t)}, device_id_type=MESH)
    pl.semaphore_wait(barrier, n_ctx + n_dp - 2)

    started = []

    def send(src, dst, send_sem, recv_sem, device):
        copy = pltpu.make_async_remote_copy(
            src_ref=src, dst_ref=dst, send_sem=send_sem, recv_sem=recv_sem,
            device_id=device, device_id_type=MESH,
        )
        copy.start()
        started.append(copy)

    def arrive(dst, send_sem, recv_sem, device):
        pltpu.make_async_remote_copy(
            src_ref=dst, dst_ref=dst, send_sem=send_sem, recv_sem=recv_sem,
            device_id=device, device_id_type=MESH,
        ).wait_recv()

    pairs = ((0, k_ref.at[0], k_all), (1, v_ref.at[0], v_all))
    n_half = n_ctx // 2
    for a, src, dst in pairs:
        for t in range(1, n_half):
            send(src, block(dst, me), kv_send.at[a, t], kv_recv.at[a, me], {"ctx": ctx_peer(2 * t)})
    for a, src, dst in pairs:
        send(src, block(dst, me), kv_send.at[a, 0], kv_recv.at[a, me], {"ctx": sibling})
    k_all[pl.ds(pl.multiple_of(me * tok, tok), tok), :] = k_ref[0]
    v_all[pl.ds(pl.multiple_of(me * tok, tok), tok), :] = v_ref[0]

    ends = []
    end = 0
    for d in range(DOCS):
        end = end + len_ref[0, d]
        ends.append(end)

    def doc_at(pos):
        doc = jnp.zeros(pos.shape, jnp.int32)
        for d in range(DOCS):
            doc = doc + (pos >= ends[d]).astype(jnp.int32)
        return doc

    first = me * tok
    q_pos = first + lax.broadcasted_iota(jnp.int32, (tok, seq), 0)
    k_pos = lax.broadcasted_iota(jnp.int32, (tok, seq), 1)
    allowed = (doc_at(q_pos) == doc_at(k_pos)) & (k_pos <= q_pos)
    bias[...] = jnp.where(allowed, 0.0, NEG)
    doc_col = doc_at(first + lax.broadcasted_iota(jnp.int32, (tok, HEAD_DIM), 0))
    wire_doc = lax.rem(lax.broadcasted_iota(jnp.int32, (WIRE, tok), 0), DOCS)
    member = (
        doc_at(first + lax.broadcasted_iota(jnp.int32, (WIRE, tok), 1)) == wire_doc
    ).astype(F32).astype(BF16)
    len_doc = lax.rem(lax.broadcasted_iota(jnp.int32, (WIRE, 1), 0), DOCS)
    doc_len = jnp.zeros((WIRE, 1), F32)
    for d in range(DOCS):
        doc_len = jnp.where(len_doc == d, len_ref[0, d].astype(F32), doc_len)
    for h in range(HEADS):
        q_s[h * tok:(h + 1) * tok, :] = q_ref[0, :, h * HEAD_DIM:(h + 1) * HEAD_DIM]
    q_sq = jnp.zeros((emb_ref.shape[0], HEAD_DIM), F32)
    for h in range(HEADS):
        part = emb_ref[:, h * HEAD_DIM:(h + 1) * HEAD_DIM].astype(F32)
        q_sq = q_sq + part * part
    q_inv = lax.rsqrt(jnp.sum(q_sq, axis=1, keepdims=True) + EPSILON)

    for a, src, dst in pairs:
        for t in range(1, n_half):
            idx = ctx_peer(2 * t)
            arrive(block(dst, idx), kv_send.at[a, t], kv_recv.at[a, idx], {"ctx": sibling})
            send(block(dst, idx), block(dst, idx), kv_send.at[a, n_half + t], kv_recv.at[a, idx],
                 {"ctx": sibling})
    for a, src, dst in pairs:
        for t in range(n_half):
            idx = lax.rem(sibling + 2 * t, n_ctx)
            arrive(block(dst, idx), kv_send.at[a, 0], kv_recv.at[a, idx], {"ctx": sibling})

    low_rows = lax.broadcasted_iota(jnp.int32, (WIRE, HEAD_DIM), 0) < DOCS

    def head_rows(g, i):
        return pl.ds(pl.multiple_of((g * PER_GROUP + i) * tok, tok), tok)

    def forward(i, carry):
        docs = []
        for g in range(KV_HEADS):
            rows = head_rows(g, i)
            k_g = k_all[:, g * HEAD_DIM:(g + 1) * HEAD_DIM]
            v_g = v_all[:, g * HEAD_DIM:(g + 1) * HEAD_DIM]
            scores = dot_nt(q_s[rows, :], k_g) * factor + bias[...]
            e = jnp.exp(scores - jnp.max(scores, axis=1, keepdims=True))
            p = e * (1.0 / jnp.sum(e, axis=1, keepdims=True))
            probs[rows, :] = p
            out = dot_nn(p.astype(BF16), v_g)
            att[rows, :] = out
            high, low = split(out)
            docs.append(dot_nn(member, high) + dot_nn(member, low))
        cols = pl.ds(pl.multiple_of(i * HEAD_DIM, HEAD_DIM), HEAD_DIM)
        sums[me, :, cols] = jnp.where(low_rows, docs[0], docs[1])
        return carry

    lax.fori_loop(0, PER_GROUP, forward, 0)
    for t in range(1, n_ctx):
        send(sums.at[me], sums.at[me], sum_send.at[t], sum_recv.at[me], {"ctx": ctx_peer(t)})
    for t in range(1, n_ctx):
        idx = ctx_peer(t)
        arrive(sums.at[idx], sum_send.at[t], sum_recv.at[idx], {"ctx": idx})
    doc_sum = sums[0]
    for c in range(1, n_ctx):
        doc_sum = doc_sum + sums[c]
    doc_emb = doc_sum / doc_len
    doc_inv = lax.rsqrt(doc_row_sum(doc_emb * doc_emb) + EPSILON)
    doc_unit = doc_emb * doc_inv
    units[row] = doc_unit
    for t in range(1, n_dp):
        send(units.at[row], units.at[row], unit_send.at[t], unit_recv.at[row], {"dp": dp_peer(t)})
    for t in range(1, n_dp):
        idx = dp_peer(t)
        arrive(units.at[idx], unit_send.at[t], unit_recv.at[idx], {"dp": idx})

    low_half = lax.broadcasted_iota(jnp.int32, (WIRE, half), 0) < DOCS
    for r in range(0, n_dp, 2):
        lefts, rights = [], []
        for s in range(2):
            w = units[r + s]
            other = swap_halves(w)
            lefts.append(jnp.where(low_half, w, other))
            rights.append(jnp.where(low_half, other, w))
        for at, x in ((0, jnp.concatenate(lefts, 0)), (half, jnp.concatenate(rights, 0))):
            high, low = split(x)
            doc_hi[r * WIRE:(r + 2) * WIRE, at:at + half] = high
            doc_lo[r * WIRE:(r + 2) * WIRE, at:at + half] = low

    q_emb = emb_ref[...]
    logits = (dot_nt(q_emb, doc_hi[...]) + dot_nt(q_emb, doc_lo[...])) * (q_inv * SCALE_UP)
    column = lax.broadcasted_iota(jnp.int32, logits.shape, 1)
    once = lax.rem(column, WIRE) < DOCS
    doc_of = (column // WIRE) * DOCS + lax.rem(column, DOCS)
    e = jnp.exp(logits)
    target = (doc_of == pos_ref[...]).astype(F32)
    coef = e / jnp.sum(jnp.where(once, e, 0.0), axis=1, keepdims=True) - target

    c_hi, c_lo = split(coef * (q_inv * SCALE_UP))
    for at in (0, half):
        part = emb_ref[:, at:at + half]
        w = dot_tn(c_hi, part) + dot_tn(c_lo, part)
        for r in range(n_dp):
            rows = w[r * WIRE:(r + 1) * WIRE]
            if at == 0:
                terms[1, r] = rows
            else:
                terms[1, r] = jnp.where(low_half, terms[1, r], rows)
    for t in range(1, n_dp):
        idx = dp_peer(t)
        send(terms.at[1, idx], terms.at[0, row], term_send.at[t], term_recv.at[row], {"dp": idx})
    terms[0, row] = terms[1, row]

    coef_once = jnp.where(once, coef, 0.0)
    inner = jnp.sum(coef_once * logits, axis=1, keepdims=True) * q_inv
    c_hi, c_lo = split(coef_once * SCALE_UP)
    step = 2 * HEAD_DIM
    for at in range(0, emb, step):
        d_hi = doc_hi[:, at:at + step]
        u = dot_nn(c_hi, d_hi) + dot_nn(c_lo, d_hi) + dot_nn(c_hi, doc_lo[:, at:at + step])
        qg_ref[:, at:at + step] = q_inv * (u - emb_ref[:, at:at + step].astype(F32) * inner)

    for t in range(1, n_dp):
        idx = dp_peer(t)
        arrive(terms.at[0, idx], term_send.at[t], term_recv.at[idx], {"dp": idx})
    w = terms[0, 0]
    for r in range(1, n_dp):
        w = w + terms[0, r]
    doc_grad[...] = doc_inv * (w - doc_unit * doc_row_sum(doc_unit * w)) / doc_len

    def backward(i, carry):
        cols = pl.ds(pl.multiple_of(i * HEAD_DIM, HEAD_DIM), HEAD_DIM)
        for g in range(KV_HEADS):
            rows = head_rows(g, i)
            og = jnp.zeros((tok, HEAD_DIM), F32)
            grads = doc_grad[:, cols]
            for d in range(DOCS):
                og = jnp.where(doc_col == d, grads[g * DOCS + d:g * DOCS + d + 1], og)
            delta = jnp.sum(og * att[rows, :], axis=1, keepdims=True)
            low = og.astype(BF16)
            out_low[rows, :] = low
            flow = dot_nt(low, v_all[:, g * HEAD_DIM:(g + 1) * HEAD_DIM])
            p = probs[rows, :]
            weights[rows, :] = p.astype(BF16)
            s_grad[rows, :] = (p * (flow - delta)).astype(BF16)
        return carry

    lax.fori_loop(0, PER_GROUP, backward, 0)

    span = PER_GROUP * tok
    for a, lhs, rhs, out, into, scale in (
        (0, weights, out_low, v_out, v_in, 1.0),
        (1, s_grad, q_s, k_out, k_in, factor),
    ):
        for g in range(KV_HEADS):
            part = dot_tn(lhs[g * span:(g + 1) * span, :], rhs[g * span:(g + 1) * span, :])
            out[:, g * HEAD_DIM:(g + 1) * HEAD_DIM] = (part * scale).astype(BF16)
        for t in range(1, n_ctx):
            idx = ctx_peer(t)
            send(block(out, idx), into.at[me], part_send.at[a, t], part_recv.at[a, me], {"ctx": idx})
        into[me] = out[pl.ds(pl.multiple_of(me * tok, tok), tok), :]

    for g in range(KV_HEADS):
        k_g = k_all[:, g * HEAD_DIM:(g + 1) * HEAD_DIM]
        for i in range(PER_GROUP):
            h = g * PER_GROUP + i
            dq = dot_nn(s_grad[h * tok:(h + 1) * tok, :], k_g) * factor
            gq_ref[0, :, h * HEAD_DIM:(h + 1) * HEAD_DIM] = dq.astype(BF16)

    for a, into, res in ((0, v_in, gv_ref), (1, k_in, gk_ref)):
        for t in range(1, n_ctx):
            idx = ctx_peer(t)
            arrive(into.at[idx], part_send.at[a, t], part_recv.at[a, idx], {"ctx": idx})
        total = into[0].astype(F32)
        for c in range(1, n_ctx):
            total = total + into[c].astype(F32)
        res[0] = total.astype(BF16)

    for copy in started:
        copy.wait_send()


def per_device(n_ctx, n_dp, queries_q, keys, values, lengths, query_emb, positive):
    tok, emb = queries_q.shape[1:]
    kv_width = keys.shape[2]
    seq = tok * n_ctx
    nq = query_emb.shape[0]
    n_rows = HEADS * tok
    half = emb // 2
    vmem = pl.BlockSpec(memory_space=pltpu.VMEM)
    dma = pltpu.SemaphoreType.DMA
    return pl.pallas_call(
        functools.partial(kernel, n_ctx, n_dp),
        out_shape=(
            jax.ShapeDtypeStruct((nq, emb), F32),
            jax.ShapeDtypeStruct(queries_q.shape, BF16),
            jax.ShapeDtypeStruct(keys.shape, BF16),
            jax.ShapeDtypeStruct(values.shape, BF16),
        ),
        in_specs=[pl.BlockSpec(memory_space=pltpu.SMEM)] + [vmem] * 5,
        out_specs=(vmem,) * 4,
        scratch_shapes=[
            pltpu.VMEM((seq, kv_width), BF16),
            pltpu.VMEM((seq, kv_width), BF16),
            pltpu.VMEM((n_rows, HEAD_DIM), BF16),
            pltpu.VMEM((n_rows, seq), F32),
            pltpu.VMEM((n_rows, HEAD_DIM), F32),
            pltpu.VMEM((tok, seq), F32),
            pltpu.VMEM((n_ctx, WIRE, half), F32),
            pltpu.VMEM((n_dp, WIRE, half), F32),
            pltpu.VMEM((2, n_dp, WIRE, half), F32),
            pltpu.VMEM((n_dp * WIRE, emb), BF16),
            pltpu.VMEM((n_dp * WIRE, emb), BF16),
            pltpu.VMEM((WIRE, half), F32),
            pltpu.VMEM((n_rows, HEAD_DIM), BF16),
            pltpu.VMEM((n_rows, seq), BF16),
            pltpu.VMEM((n_rows, seq), BF16),
            pltpu.VMEM((seq, kv_width), BF16),
            pltpu.VMEM((seq, kv_width), BF16),
            pltpu.VMEM((n_ctx, tok, kv_width), BF16),
            pltpu.VMEM((n_ctx, tok, kv_width), BF16),
            dma((2, n_ctx)), dma((2, n_ctx)),
            dma((n_ctx,)), dma((n_ctx,)),
            dma((n_dp,)), dma((n_dp,)),
            dma((n_dp,)), dma((n_dp,)),
            dma((2, n_ctx)), dma((2, n_ctx)),
        ],
        compiler_params=pltpu.CompilerParams(
            collective_id=0, has_side_effects=True, vmem_limit_bytes=56 * 1024 * 1024
        ),
    )(lengths, queries_q, keys, values, query_emb, positive[:, None])


def solution(mesh):
    placed = (
        P("dp", "ctx", None),
        P("dp", "ctx", None),
        P("dp", "ctx", None),
        P("dp", None),
        P("dp", None),
        P("dp"),
    )
    return jax.shard_map(
        functools.partial(per_device, mesh.shape["ctx"], mesh.shape["dp"]),
        mesh=mesh,
        in_specs=placed,
        out_specs=(P("dp", None), P("dp", "ctx", None), P("dp", "ctx", None), P("dp", "ctx", None)),
        check_vma=False,
    )
```

```python
import functools

import jax
import jax.numpy as jnp
from jax import lax
from jax.experimental import pallas as pl
from jax.experimental.pallas import tpu as pltpu
from jax.sharding import PartitionSpec as P

HEAD_DIM = 128
HEADS = 14
KV_HEADS = 2
PER_GROUP = HEADS // KV_HEADS
DOCS = 4
WIRE = KV_HEADS * DOCS

SCALE_UP = 20.0
EPSILON = 1e-06
NEG = -1e30
F32 = jnp.float32
BF16 = jnp.bfloat16
MESH = pl.DeviceIdType.MESH


def dot_nn(a, b):
    return lax.dot_general(a, b, (((1,), (0,)), ((), ())), preferred_element_type=F32)


def dot_nt(a, b):
    return lax.dot_general(a, b, (((1,), (1,)), ((), ())), preferred_element_type=F32)


def dot_tn(a, b):
    return lax.dot_general(a, b, (((0,), (0,)), ((), ())), preferred_element_type=F32)


def split(x):
    high = x.astype(BF16)
    return high, (x - high.astype(F32)).astype(BF16)


def swap_halves(x):
    return jnp.concatenate([x[DOCS:], x[:DOCS]], axis=0)


def doc_row_sum(x):
    rows = jnp.sum(x, axis=1, keepdims=True)
    return rows + swap_halves(rows)


def kernel(
    n_ctx, n_dp,
    len_ref, q_ref, k_ref, v_ref, emb_ref, pos_ref,
    qg_ref, gq_ref, gk_ref, gv_ref,
    k_all, v_all, q_s, probs, att, bias, sums, units, terms, doc_hi, doc_lo,
    doc_grad, col_sums, flows, s_grad, k_out, v_out, k_in, v_in, pair,
    kv_send, kv_recv, sum_send, sum_recv, unit_send, unit_recv, unit_relay, term_send, term_recv,
    pair_send, pair_recv, part_send, part_recv,
):
    me = lax.axis_index("ctx")
    row = lax.axis_index("dp")
    tok = q_ref.shape[1]
    seq = k_all.shape[0]
    emb = q_ref.shape[2]
    half = emb // 2
    factor = HEAD_DIM ** (-0.5)
    core = lax.rem(me, 2)
    sibling = me + 1 - 2 * core

    def ctx_peer(t):
        return lax.rem(me + t, n_ctx)

    def dp_peer(t):
        return lax.rem(row + t, n_dp)

    def each_row(parity, action):
        for u in range(n_dp // 2):
            t = 2 * u + 1 + parity
            if 2 * u + 2 < n_dp:
                action(u, t)
            else:
                pl.when(parity == 0)(functools.partial(action, u, t))

    def block(ref, idx):
        return ref.at[pl.ds(pl.multiple_of(idx * tok, tok), tok)]

    barrier = pltpu.get_barrier_semaphore()
    for t in range(1, n_ctx):
        pl.semaphore_signal(barrier, inc=1, device_id={"ctx": ctx_peer(t)}, device_id_type=MESH)
    for t in range(1, n_dp):
        pl.semaphore_signal(barrier, inc=1, device_id={"dp": dp_peer(t)}, device_id_type=MESH)
    pl.semaphore_wait(barrier, n_ctx + n_dp - 2)

    started = []

    def send(src, dst, send_sem, recv_sem, device):
        copy = pltpu.make_async_remote_copy(
            src_ref=src, dst_ref=dst, send_sem=send_sem, recv_sem=recv_sem,
            device_id=device, device_id_type=MESH,
        )
        copy.start()
        started.append(copy)
        return copy

    def arrive(dst, send_sem, recv_sem, device):
        pltpu.make_async_remote_copy(
            src_ref=dst, dst_ref=dst, send_sem=send_sem, recv_sem=recv_sem,
            device_id=device, device_id_type=MESH,
        ).wait_recv()

    pairs = ((0, k_ref.at[0], k_all), (1, v_ref.at[0], v_all))
    n_half = n_ctx // 2
    for a, src, dst in pairs:
        for t in range(1, n_half):
            send(src, block(dst, me), kv_send.at[a, t], kv_recv.at[a, me], {"ctx": ctx_peer(2 * t)})
    for a, src, dst in pairs:
        send(src, block(dst, me), kv_send.at[a, 0], kv_recv.at[a, me], {"ctx": sibling})
    k_all[pl.ds(pl.multiple_of(me * tok, tok), tok), :] = k_ref[0]
    v_all[pl.ds(pl.multiple_of(me * tok, tok), tok), :] = v_ref[0]

    ends = []
    end = 0
    for d in range(DOCS):
        end = end + len_ref[0, d]
        ends.append(end)

    def doc_at(pos):
        doc = jnp.zeros(pos.shape, jnp.int32)
        for d in range(DOCS):
            doc = doc + (pos >= ends[d]).astype(jnp.int32)
        return doc

    first = me * tok
    q_pos = first + lax.broadcasted_iota(jnp.int32, (tok, seq), 0)
    k_pos = lax.broadcasted_iota(jnp.int32, (tok, seq), 1)
    allowed = (doc_at(q_pos) == doc_at(k_pos)) & (k_pos <= q_pos)
    bias[...] = jnp.where(allowed, 0.0, NEG)
    doc_col = doc_at(first + lax.broadcasted_iota(jnp.int32, (tok, HEAD_DIM), 0))
    wire_doc = lax.rem(lax.broadcasted_iota(jnp.int32, (WIRE, tok), 0), DOCS)
    member = (
        doc_at(first + lax.broadcasted_iota(jnp.int32, (WIRE, tok), 1)) == wire_doc
    ).astype(F32).astype(BF16)
    len_doc = lax.rem(lax.broadcasted_iota(jnp.int32, (WIRE, 1), 0), DOCS)
    doc_len = jnp.zeros((WIRE, 1), F32)
    for d in range(DOCS):
        doc_len = jnp.where(len_doc == d, len_ref[0, d].astype(F32), doc_len)
    k_mask = (
        doc_at(lax.broadcasted_iota(jnp.int32, (WIRE, seq), 1))
        == lax.rem(lax.broadcasted_iota(jnp.int32, (WIRE, seq), 0), DOCS)
    ).astype(F32)
    low_keys = lax.broadcasted_iota(jnp.int32, (WIRE, seq), 0) < DOCS
    col_sums[PER_GROUP * WIRE:, :] = jnp.zeros((WIRE, seq), F32)
    for h in range(HEADS):
        q_s[h * tok:(h + 1) * tok, :] = q_ref[0, :, h * HEAD_DIM:(h + 1) * HEAD_DIM]
    nq = emb_ref.shape[0]
    diagonal = lax.broadcasted_iota(jnp.int32, (nq, nq), 0) == lax.broadcasted_iota(
        jnp.int32, (nq, nq), 1
    )
    positive = jnp.sum(
        jnp.where(diagonal, pos_ref[...].astype(F32), 0.0), axis=1, keepdims=True
    ).astype(jnp.int32)
    q_sq = jnp.zeros((emb_ref.shape[0], HEAD_DIM), F32)
    for h in range(HEADS):
        part = emb_ref[:, h * HEAD_DIM:(h + 1) * HEAD_DIM].astype(F32)
        q_sq = q_sq + part * part
    q_inv = lax.rsqrt(jnp.sum(q_sq, axis=1, keepdims=True) + EPSILON)

    for a, src, dst in pairs:
        for t in range(1, n_half):
            idx = ctx_peer(2 * t)
            arrive(block(dst, idx), kv_send.at[a, t], kv_recv.at[a, idx], {"ctx": sibling})
            send(block(dst, idx), block(dst, idx), kv_send.at[a, n_half + t], kv_recv.at[a, idx],
                 {"ctx": sibling})
    for a, src, dst in pairs:
        for t in range(n_half):
            idx = lax.rem(sibling + 2 * t, n_ctx)
            arrive(block(dst, idx), kv_send.at[a, 0], kv_recv.at[a, idx], {"ctx": sibling})

    low_rows = lax.broadcasted_iota(jnp.int32, (WIRE, HEAD_DIM), 0) < DOCS

    def head_rows(g, i):
        return pl.ds(pl.multiple_of((g * PER_GROUP + i) * tok, tok), tok)

    def forward(i, carry):
        docs, cols_of = [], []
        for g in range(KV_HEADS):
            rows = head_rows(g, i)
            k_g = k_all[:, g * HEAD_DIM:(g + 1) * HEAD_DIM]
            v_g = v_all[:, g * HEAD_DIM:(g + 1) * HEAD_DIM]
            scores = dot_nt(q_s[rows, :], k_g) * factor + bias[...]
            e = jnp.exp(scores - jnp.max(scores, axis=1, keepdims=True))
            p = e * (1.0 / jnp.sum(e, axis=1, keepdims=True))
            probs[rows, :] = p
            low = p.astype(BF16)
            cols_of.append(jnp.sum(low.astype(F32), axis=0, keepdims=True))
            out = dot_nn(low, v_g)
            att[rows, :] = out
            out_hi, out_lo = split(out)
            docs.append(dot_nn(member, out_hi) + dot_nn(member, out_lo))
        wire_rows = pl.ds(pl.multiple_of(i * WIRE, WIRE), WIRE)
        col_sums[wire_rows, :] = jnp.where(low_keys, cols_of[0], cols_of[1]) * k_mask
        cols = pl.ds(pl.multiple_of(i * HEAD_DIM, HEAD_DIM), HEAD_DIM)
        sums[me, :, cols] = jnp.where(low_rows, docs[0], docs[1])
        return carry

    lax.fori_loop(0, PER_GROUP, forward, 0, unroll=True)
    for t in range(1, n_ctx):
        send(sums.at[me], sums.at[me], sum_send.at[t], sum_recv.at[me], {"ctx": ctx_peer(t)})
    for t in range(1, n_ctx):
        idx = ctx_peer(t)
        arrive(sums.at[idx], sum_send.at[t], sum_recv.at[idx], {"ctx": idx})
    doc_sum = sums[0]
    for c in range(1, n_ctx):
        doc_sum = doc_sum + sums[c]
    doc_emb = doc_sum / doc_len
    doc_inv = lax.rsqrt(doc_row_sum(doc_emb * doc_emb) + EPSILON)
    doc_unit = doc_emb * doc_inv
    units[row] = doc_unit
    def send_unit(u, t):
        send(units.at[row], units.at[row], unit_send.at[u], unit_recv.at[row], {"dp": dp_peer(t)})

    def relay_unit(u, t):
        idx = dp_peer(n_dp - t)
        arrive(units.at[idx], unit_send.at[u], unit_recv.at[idx], {"dp": idx})
        send(units.at[idx], units.at[idx], unit_relay.at[u], unit_recv.at[idx], {"ctx": sibling})

    def take_unit(u, t):
        idx = dp_peer(n_dp - t)
        arrive(units.at[idx], unit_relay.at[u], unit_recv.at[idx], {"ctx": sibling})

    def sent_unit(u, t):
        for sem in (unit_send.at[u], unit_relay.at[u]):
            pltpu.make_async_remote_copy(
                src_ref=units.at[row], dst_ref=units.at[row], send_sem=sem,
                recv_sem=unit_recv.at[row], device_id={"ctx": sibling}, device_id_type=MESH,
            ).wait_send()

    kept = len(started)
    each_row(core, send_unit)
    each_row(core, relay_unit)
    each_row(1 - core, take_unit)
    del started[kept:]

    low_half = lax.broadcasted_iota(jnp.int32, (WIRE, half), 0) < DOCS
    for r in range(0, n_dp, 2):
        lefts, rights = [], []
        for s in range(2):
            w = units[r + s]
            other = swap_halves(w)
            lefts.append(jnp.where(low_half, w, other))
            rights.append(jnp.where(low_half, other, w))
        for at, x in ((0, jnp.concatenate(lefts, 0)), (half, jnp.concatenate(rights, 0))):
            high, low = split(x)
            doc_hi[r * WIRE:(r + 2) * WIRE, at:at + half] = high
            doc_lo[r * WIRE:(r + 2) * WIRE, at:at + half] = low

    q_emb = emb_ref[...]
    logits = (dot_nt(q_emb, doc_hi[...]) + dot_nt(q_emb, doc_lo[...])) * (q_inv * SCALE_UP)
    column = lax.broadcasted_iota(jnp.int32, logits.shape, 1)
    once = lax.rem(column, WIRE) < DOCS
    doc_of = (column // WIRE) * DOCS + lax.rem(column, DOCS)
    e = jnp.exp(logits)
    target = (doc_of == positive).astype(F32)
    coef = e / jnp.sum(jnp.where(once, e, 0.0), axis=1, keepdims=True) - target

    c_hi, c_lo = split(coef * (q_inv * SCALE_UP))
    for at in (0, half):
        part = emb_ref[:, at:at + half]
        w = dot_tn(c_hi, part) + dot_tn(c_lo, part)
        for r in range(n_dp):
            rows = w[r * WIRE:(r + 1) * WIRE]
            if at == 0:
                terms[1, r] = rows
            else:
                terms[1, r] = jnp.where(low_half, terms[1, r], rows)
    def send_term(u, t):
        idx = dp_peer(t)
        send(terms.at[1, idx], terms.at[0, row], term_send.at[u], term_recv.at[row], {"dp": idx})

    def take_term(u, t):
        idx = dp_peer(n_dp - t)
        arrive(terms.at[0, idx], term_send.at[u], term_recv.at[idx], {"dp": idx})
        pair[core] += terms[0, idx]

    def sent_term(u, t):
        pltpu.make_async_remote_copy(
            src_ref=terms.at[1, row], dst_ref=terms.at[0, row], send_sem=term_send.at[u],
            recv_sem=term_recv.at[row], device_id={"ctx": sibling}, device_id_type=MESH,
        ).wait_send()

    kept = len(started)
    each_row(core, send_term)
    del started[kept:]

    coef_once = jnp.where(once, coef, 0.0)
    inner = jnp.sum(coef_once * logits, axis=1, keepdims=True) * q_inv
    c_hi, c_lo = split(coef_once * SCALE_UP)
    step = 2 * HEAD_DIM
    for at in range(0, emb, step):
        d_hi = doc_hi[:, at:at + step]
        u = dot_nn(c_hi, d_hi) + dot_nn(c_lo, d_hi) + dot_nn(c_hi, doc_lo[:, at:at + step])
        qg_ref[:, at:at + step] = q_inv * (u - emb_ref[:, at:at + step].astype(F32) * inner)

    pair[core] = jnp.zeros((WIRE, half), F32)
    each_row(core, take_term)
    send(pair.at[core], pair.at[core], pair_send, pair_recv, {"ctx": sibling})
    arrive(pair.at[1 - core], pair_send, pair_recv, {"ctx": sibling})
    w = terms[1, row] + (pair[0] + pair[1])
    doc_grad[...] = doc_inv * (w - doc_unit * doc_row_sum(doc_unit * w)) / doc_len

    def send_parts(a, out, into):
        for t in range(1, n_ctx):
            idx = ctx_peer(t)
            send(block(out, idx), into.at[me], part_send.at[a, t], part_recv.at[a, me], {"ctx": idx})
        into[me] = out[pl.ds(pl.multiple_of(me * tok, tok), tok), :]

    low = jnp.concatenate(
        [doc_grad[:, i * HEAD_DIM:(i + 1) * HEAD_DIM] for i in range(PER_GROUP)]
        + [jnp.zeros((WIRE, HEAD_DIM), F32)], axis=0
    )
    low_docs = lax.rem(lax.broadcasted_iota(jnp.int32, low.shape, 0), WIRE) < DOCS
    low_parts = jnp.concatenate(
        [jnp.where(low_docs, low, 0.0), jnp.where(low_docs, 0.0, low)], axis=1
    ).astype(BF16)
    s_hi, s_lo = split(col_sums[...])
    v_out[...] = (dot_tn(s_hi, low_parts) + dot_tn(s_lo, low_parts)).astype(BF16)
    send_parts(0, v_out, v_in)
    flows[...] = dot_nt(low_parts, v_all[...])

    def backward(i, carry):
        cols = pl.ds(pl.multiple_of(i * HEAD_DIM, HEAD_DIM), HEAD_DIM)
        grads = doc_grad[:, cols]
        flow_rows = flows[pl.ds(pl.multiple_of(i * WIRE, WIRE), WIRE), :] * k_mask
        for g in range(KV_HEADS):
            rows = head_rows(g, i)
            og = jnp.zeros((tok, HEAD_DIM), F32)
            for d in range(DOCS):
                og = jnp.where(doc_col == d, grads[g * DOCS + d:g * DOCS + d + 1], og)
            delta = jnp.sum(og * att[rows, :], axis=1, keepdims=True)
            flow = jnp.sum(flow_rows[g * DOCS:(g + 1) * DOCS], axis=0, keepdims=True)
            s_grad[rows, :] = (probs[rows, :] * (flow - delta)).astype(BF16)
        return carry

    lax.fori_loop(0, PER_GROUP, backward, 0, unroll=True)

    span = PER_GROUP * tok
    for g in range(KV_HEADS):
        part = dot_tn(s_grad[g * span:(g + 1) * span, :], q_s[g * span:(g + 1) * span, :])
        k_out[:, g * HEAD_DIM:(g + 1) * HEAD_DIM] = (part * factor).astype(BF16)
    send_parts(1, k_out, k_in)

    for g in range(KV_HEADS):
        k_g = k_all[:, g * HEAD_DIM:(g + 1) * HEAD_DIM]
        for i in range(PER_GROUP):
            h = g * PER_GROUP + i
            dq = dot_nn(s_grad[h * tok:(h + 1) * tok, :], k_g) * factor
            gq_ref[0, :, h * HEAD_DIM:(h + 1) * HEAD_DIM] = dq.astype(BF16)

    for a, into, res in ((0, v_in, gv_ref), (1, k_in, gk_ref)):
        for t in range(1, n_ctx):
            idx = ctx_peer(t)
            arrive(into.at[idx], part_send.at[a, t], part_recv.at[a, idx], {"ctx": idx})
        total = into[0].astype(F32)
        for c in range(1, n_ctx):
            total = total + into[c].astype(F32)
        res[0] = total.astype(BF16)

    for copy in started:
        copy.wait_send()
    each_row(core, sent_unit)
    each_row(core, sent_term)


def per_device(n_ctx, n_dp, queries_q, keys, values, lengths, query_emb, positive):
    tok, emb = queries_q.shape[1:]
    kv_width = keys.shape[2]
    seq = tok * n_ctx
    nq = query_emb.shape[0]
    n_rows = HEADS * tok
    half = emb // 2
    vmem = pl.BlockSpec(memory_space=pltpu.VMEM)
    dma = pltpu.SemaphoreType.DMA
    return pl.pallas_call(
        functools.partial(kernel, n_ctx, n_dp),
        out_shape=(
            jax.ShapeDtypeStruct((nq, emb), F32),
            jax.ShapeDtypeStruct(queries_q.shape, BF16),
            jax.ShapeDtypeStruct(keys.shape, BF16),
            jax.ShapeDtypeStruct(values.shape, BF16),
        ),
        in_specs=[pl.BlockSpec(memory_space=pltpu.SMEM)] + [vmem] * 5,
        out_specs=(vmem,) * 4,
        scratch_shapes=[
            pltpu.VMEM((seq, kv_width), BF16),
            pltpu.VMEM((seq, kv_width), BF16),
            pltpu.VMEM((n_rows, HEAD_DIM), BF16),
            pltpu.VMEM((n_rows, seq), F32),
            pltpu.VMEM((n_rows, HEAD_DIM), F32),
            pltpu.VMEM((tok, seq), F32),
            pltpu.VMEM((n_ctx, WIRE, half), F32),
            pltpu.VMEM((n_dp, WIRE, half), F32),
            pltpu.VMEM((2, n_dp, WIRE, half), F32),
            pltpu.VMEM((n_dp * WIRE, emb), BF16),
            pltpu.VMEM((n_dp * WIRE, emb), BF16),
            pltpu.VMEM((WIRE, half), F32),
            pltpu.VMEM(((PER_GROUP + 1) * WIRE, seq), F32),
            pltpu.VMEM(((PER_GROUP + 1) * WIRE, seq), F32),
            pltpu.VMEM((n_rows, seq), BF16),
            pltpu.VMEM((seq, kv_width), BF16),
            pltpu.VMEM((seq, kv_width), BF16),
            pltpu.VMEM((n_ctx, tok, kv_width), BF16),
            pltpu.VMEM((n_ctx, tok, kv_width), BF16),
            pltpu.VMEM((2, WIRE, half), F32),
            dma((2, n_ctx)), dma((2, n_ctx)),
            dma((n_ctx,)), dma((n_ctx,)),
            dma((n_dp // 2,)), dma((n_dp,)), dma((n_dp // 2,)),
            dma((n_dp // 2,)), dma((n_dp,)),
            dma(()), dma(()),
            dma((2, n_ctx)), dma((2, n_ctx)),
        ],
        compiler_params=pltpu.CompilerParams(
            collective_id=0, has_side_effects=True, vmem_limit_bytes=56 * 1024 * 1024
        ),
    )(lengths, queries_q, keys, values, query_emb, positive[None, :])


def solution(mesh):
    placed = (
        P("dp", "ctx", None),
        P("dp", "ctx", None),
        P("dp", "ctx", None),
        P("dp", None),
        P("dp", None),
        P("dp"),
    )
    return jax.shard_map(
        functools.partial(per_device, mesh.shape["ctx"], mesh.shape["dp"]),
        mesh=mesh,
        in_specs=placed,
        out_specs=(P("dp", None), P("dp", "ctx", None), P("dp", "ctx", None), P("dp", "ctx", None)),
        check_vma=False,
    )
```
